512 devices in a mesh: fsdp: 64 (over z_hi, y, x), sp: 8 (over z_lo, core).
Axes of the slice: x: 4, y: 4, z: 16 (z_hi: 4, z_lo: 4; z = z_hi * 4 + z_lo), core: 2. Of those that a mesh axis runs over, the one named last changes fastest.
Arguments:
- latents: bfloat16 [64, 192, 3072], P('fsdp', 'sp'), may hold values from -6 to 6
- step_noise: bfloat16 [64, 192, 3072], P('fsdp', 'sp'), may hold values from -6 to 6
- base_qkv: bfloat16 [3, 3072, 3072], P(None, 'fsdp', 'sp'), may hold values from -1 to 1
- down_qkv: bfloat16 [3, 3072, 64], P(None, 'fsdp'), may hold values from -0.109375 to 0.109375
- up_query_key_value: bfloat16 [3, 64, 3072], P(None, None, 'sp'), may hold values from -0.625 to 0.625
- base_out: bfloat16 [3072, 3072], P('sp', 'fsdp'), may hold values from -0.109375 to 0.109375
- down_out: bfloat16 [3072, 64], P('sp'), may hold values from -0.109375 to 0.109375
- up_out: bfloat16 [64, 3072], P(None, 'fsdp'), may hold values from -0.625 to 0.625
- modulation: float32 [16, 3, 3072], replicated, may hold values from -3 to 3
- timestep: int32 [64], P('fsdp'), may hold values from 0 to 14
Outputs:
- velocity: bfloat16 [64, 192, 3072], P('fsdp', 'sp')
- next_latents: bfloat16 [64, 192, 3072], P('fsdp', 'sp')
The draws below stay inside these ranges and needn't reach their ends.
Inputs may be any that keep to these rules, and one draw needn't show every extreme that they name: timestep[n] + 1 is also a step of the plan.
All inputs are finite; a program needn't handle non-finite values.
Results may differ from the reference program's by a relative error of at most 0.02.
Values may be sent and summed in bfloat16 or wider, within the bound.
No kernel may reach another device: no remote copies, remote signals or barrier semaphores. Data moves between devices by JAX's collectives and lax.ppermute only.
A program may use at most 64 MiB of HBM per device.

```python
import math
import jax
import jax.numpy as jnp
from jax import lax

HEADS = 24
HEAD_DIM = 128
D = 3072
RANK = 64
NSTEP = 16
LEN = 192
SAMPLES = 64
N_SP = 8


def draw_base_qkv(key, part):
    key = jax.random.fold_in(key, 11)
    first = jax.random.fold_in(key, 0)
    columns = HEADS * HEAD_DIM
    stacked = jnp.clip(jax.random.normal(first, (3, D, columns), jnp.float32), -4.0, 4.0) / math.sqrt(D)
    return jnp.clip(stacked, -0.9, 0.9).astype(jnp.bfloat16)


def touch_ends(result, rng, least, high):
    shape = result.shape
    spot = [jax.random.randint(jax.random.fold_in(rng, axis), (), 0, shape[axis]) for axis in range(len(shape))]
    result = result.at[tuple(spot)].set(least)
    longest = shape.index(max(shape))
    spot[longest] = (spot[longest] + 1) % shape[longest]
    return result.at[tuple(spot)].set(high)


def levels(own_key, extent, pieces, least, largest):
    def one(axis_at, parts):
        draws = jax.random.uniform(jax.random.fold_in(jax.random.fold_in(own_key, 6), axis_at), (parts,), jnp.float32, least / len(pieces), largest / len(pieces))
        return jnp.repeat(jnp.exp(draws), extent[axis_at] // parts).reshape((-1,) + (1,) * (len(extent) - axis_at - 1))

    factor_of = one(*pieces[0])
    for cut in pieces[1:]:
        factor_of = factor_of * one(*cut)
    return factor_of


def scatter_about(rng, dims, scale, most, pieces=(), dtype=jnp.bfloat16):
    entries = scale * jax.random.normal(rng, dims, jnp.float32)
    if pieces:
        entries = entries * levels(rng, dims, pieces, -0.22, 0.18)
    return jnp.clip(entries, -most, most).astype(dtype)


def setup_inputs(seed: int = 0) -> dict:
    seeds = jax.random.split(jax.random.key(seed), 11)
    return {
        "latents": scatter_about(seeds[0], (SAMPLES, LEN, D), 1.0, 6.0, ((0, 64), (1, 8))),
        "step_noise": scatter_about(seeds[1], (SAMPLES, LEN, D), 1.0, 6.0, ((0, 64), (1, 8))),
        "base_qkv": draw_base_qkv(jax.random.fold_in(seeds[10], 71), 0),
        "down_qkv": scatter_about(seeds[3], (3, D, RANK), D ** -0.5, 0.109375, ((1, 64),)),
        "up_query_key_value": scatter_about(seeds[4], (3, RANK, HEADS * HEAD_DIM), 0.04, 0.625, ((2, 8),)),
        "base_out": scatter_about(seeds[5], (HEADS * HEAD_DIM, D), (HEADS * HEAD_DIM) ** -0.5, 0.109375, ((0, 8), (1, 64))),
        "down_out": scatter_about(seeds[6], (HEADS * HEAD_DIM, RANK), (HEADS * HEAD_DIM) ** -0.5, 0.109375, ((0, 8),)),
        "up_out": scatter_about(seeds[7], (RANK, D), 0.04, 0.625, ((1, 64),)),
        "modulation": scatter_about(seeds[8], (NSTEP, 3, D), 0.5, 3.0, (), jnp.float32),
        "timestep": touch_ends(jax.random.randint(seeds[9], (SAMPLES,), 0, NSTEP - 1), jax.random.fold_in(seeds[9], 1), 0, (NSTEP - 1) - 1).astype(jnp.int32),
    }


EPSILON = 1e-06
SHIFT_FACTOR = 5.0
NOISE_LEVEL = 0.7

def plan_sigma(position):
    ramp = 1.0 - position / NSTEP
    return SHIFT_FACTOR * ramp / (1.0 + (SHIFT_FACTOR - 1.0) * ramp)

def reference(latents, step_noise, base_qkv, down_qkv, up_query_key_value, base_out, down_out, up_out, modulation, timestep):
    merged_qkv = (base_qkv.astype(jnp.float32) + jnp.einsum('pdr,prc->pdc', down_qkv.astype(jnp.float32), up_query_key_value.astype(jnp.float32))).astype(jnp.bfloat16)
    merged_out = (base_out.astype(jnp.float32) + jnp.dot(down_out, up_out, preferred_element_type=jnp.float32)).astype(jnp.bfloat16)
    group_cols = HEADS * HEAD_DIM // N_SP
    grouped_output = merged_out.astype(jnp.float32).reshape(N_SP, group_cols, D)

    def one_sample(packed):
        latent, noise_rows, step_index = packed
        mod_rows = lax.dynamic_index_in_dim(modulation, step_index, 0, keepdims=False)
        latent_f = latent.astype(jnp.float32)
        mean_square = lax.optimization_barrier(jnp.mean(latent_f * latent_f, axis=-1, keepdims=True))
        normalized_rows = (latent_f * lax.rsqrt(mean_square + EPSILON) * (1.0 + mod_rows[1]) + mod_rows[0]).astype(jnp.bfloat16)
        projected = jnp.einsum('ld,pdc->plc', normalized_rows.astype(jnp.float32), merged_qkv.astype(jnp.float32)).astype(jnp.bfloat16)
        split_heads = projected.reshape(3, LEN, HEADS, HEAD_DIM).transpose(0, 2, 1, 3).astype(jnp.float32)
        scores = jnp.einsum('hqe,hke->hqk', split_heads[0], split_heads[1]) * (1.0 / HEAD_DIM ** 0.5)
        attention_weights = jax.nn.softmax(scores, axis=-1).astype(jnp.bfloat16)
        attention_result = jnp.einsum('hqk,hke->hqe', attention_weights.astype(jnp.float32), split_heads[2]).astype(jnp.bfloat16)
        attention_result = attention_result.transpose(1, 0, 2).reshape(LEN, N_SP, group_cols).astype(jnp.float32)
        partial_sums = jnp.einsum('tmy,mya->mta', attention_result, grouped_output).astype(jnp.bfloat16)
        block_out = lax.optimization_barrier(jnp.sum(partial_sums.astype(jnp.float32), axis=0))
        velocity = ((1.0 + mod_rows[2]) * block_out).astype(jnp.bfloat16)
        position = step_index.astype(jnp.float32)
        step_size = plan_sigma(position + 1.0) - plan_sigma(position)
        next_rows = latent_f + step_size * velocity.astype(jnp.float32) + NOISE_LEVEL * jnp.sqrt(-step_size) * noise_rows.astype(jnp.float32)
        return (velocity, next_rows.astype(jnp.bfloat16))
    velocity, next_latents = lax.map(one_sample, (latents, step_noise, timestep))
    return (velocity, next_latents)
```

```python
import jax
import jax.numpy as jnp
from jax import lax
from jax.sharding import PartitionSpec as P

HEAD_DIM = 128
NSTEP = 16
QUAD = 4


EPSILON = 1e-06
SHIFT_FACTOR = 5.0
NOISE_LEVEL = 0.7


def plan_sigma(position):
    ramp = 1.0 - position / NSTEP
    return SHIFT_FACTOR * ramp / (1.0 + (SHIFT_FACTOR - 1.0) * ramp)


def fsdp_index(z, y, x):
    return ((z % QUAD) * QUAD + y % QUAD) * QUAD + x % QUAD


Y_GROUPS = [[fsdp_index(z, y, x) for y in range(QUAD)] for z in range(QUAD) for x in range(QUAD)]


def shift_fsdp(value, dz=0, dx=0):
    pairs = [
        (fsdp_index(z, y, x), fsdp_index(z + dz, y, x + dx))
        for z in range(QUAD)
        for y in range(QUAD)
        for x in range(QUAD)
    ]
    return lax.ppermute(value, "fsdp", pairs)


def shift_run(value, dz):
    pairs = [
        (z * 2 + core, ((z + dz) % QUAD) * 2 + core) for z in range(QUAD) for core in range(2)
    ]
    return lax.ppermute(value, "sp", pairs)


def other_core(value):
    return lax.ppermute(value, "sp", [(i, i ^ 1) for i in range(2 * QUAD)])


def exchange_y(value):
    return lax.all_to_all(value, "fsdp", 0, 0, axis_index_groups=Y_GROUPS, tiled=True)


def per_device(
    latents,
    step_noise,
    base_qkv,
    down_qkv,
    up_query_key_value,
    base_out,
    down_out,
    up_out,
    modulation,
    timestep,
):
    z_hi = lax.axis_index("fsdp") // (QUAD * QUAD)
    x = lax.axis_index("fsdp") % QUAD
    rows, width = latents.shape[1:]
    part = base_qkv.shape[1]
    head_cols = base_qkv.shape[2]
    heads_here = head_cols // HEAD_DIM
    seq_len = rows * 2 * QUAD
    slab = width // QUAD

    lowrank = jnp.einsum(
        "prk,pkc->prc", down_qkv, up_query_key_value, preferred_element_type=jnp.float32
    )
    merged_qkv = (base_qkv.astype(jnp.float32) + lowrank).astype(jnp.bfloat16)
    lowrank_out = jnp.einsum("rk,kc->cr", down_out, up_out, preferred_element_type=jnp.float32)
    merged_out = (base_out.T.astype(jnp.float32) + lowrank_out).astype(jnp.bfloat16)
    merged = jnp.concatenate([merged_qkv, merged_out[None]], axis=0)

    def place(buffer, block, axis, index):
        start = [jnp.int32(0)] * buffer.ndim
        start[axis] = index.astype(jnp.int32)
        return lax.dynamic_update_slice(buffer, jnp.expand_dims(block, axis), start)

    held = jnp.zeros((4, QUAD, part, head_cols), jnp.bfloat16)
    for k in range(QUAD):
        block = merged if k == 0 else shift_fsdp(merged, dz=k)
        held = place(held, block, 1, (z_hi - k) % QUAD)
    weights = jnp.zeros((4, QUAD, QUAD, part, head_cols), jnp.bfloat16)
    for k in range(QUAD):
        block = held if k == 0 else shift_fsdp(held, dx=k)
        weights = place(weights, block, 2, (x - k) % QUAD)
    weights = weights.reshape(4, slab, head_cols)

    step_index = timestep[0]
    mod_rows = lax.dynamic_index_in_dim(modulation, step_index, 0, keepdims=False)
    latent_f = latents[0].astype(jnp.float32)
    mean_square = jnp.mean(latent_f * latent_f, axis=-1, keepdims=True)
    normalized_rows = (
        latent_f * lax.rsqrt(mean_square + EPSILON) * (1.0 + mod_rows[1]) + mod_rows[0]
    ).astype(jnp.bfloat16)
    slices = normalized_rows.reshape(rows, QUAD, QUAD, slab // QUAD).transpose(2, 0, 1, 3)
    mine = exchange_y(slices.reshape(QUAD, rows, slab))
    run = jnp.stack([mine] + [shift_run(mine, k) for k in range(1, QUAD)], axis=1)
    both = jnp.stack([run, other_core(run)], axis=2)
    tokens = both.reshape(QUAD * seq_len, slab)

    partial = jnp.stack(
        [
            jnp.dot(tokens, weights[p], preferred_element_type=jnp.float32)
            .astype(jnp.bfloat16)
            .reshape(QUAD, seq_len, head_cols)
            for p in range(3)
        ],
        axis=1,
    )
    projected = jnp.sum(exchange_y(partial).astype(jnp.float32), axis=0).astype(jnp.bfloat16)
    heads = projected.reshape(3, seq_len, heads_here, HEAD_DIM).transpose(0, 2, 1, 3)
    scores = jnp.einsum("hqe,hke->hqk", heads[0], heads[1], preferred_element_type=jnp.float32)
    attention_weights = jax.nn.softmax(scores * (1.0 / HEAD_DIM**0.5), axis=-1).astype(jnp.bfloat16)
    attended = jnp.einsum(
        "hqk,hke->qhe", attention_weights, heads[2], preferred_element_type=jnp.float32
    ).astype(jnp.bfloat16)
    attended = attended.reshape(seq_len, head_cols)

    gathered = lax.all_gather(attended, "fsdp", axis_index_groups=Y_GROUPS, axis=0, tiled=True)
    out_partial = lax.dot_general(
        gathered, weights[3], (((1,), (1,)), ((), ())), preferred_element_type=jnp.float32
    ).reshape(QUAD, QUAD, 2, rows, slab)
    pair = out_partial[:, :, 0] + other_core(out_partial[:, :, 1].astype(jnp.bfloat16)).astype(
        jnp.float32
    )
    total = pair[:, 0]
    for k in range(1, QUAD):
        total = total + shift_run(pair[:, k].astype(jnp.bfloat16), -k).astype(jnp.float32)
    columns = exchange_y(total.astype(jnp.bfloat16))
    block_out = (
        columns.reshape(QUAD, rows, QUAD, slab // QUAD)
        .transpose(1, 2, 0, 3)
        .reshape(rows, width)
        .astype(jnp.float32)
    )

    velocity = ((1.0 + mod_rows[2]) * block_out).astype(jnp.bfloat16)
    position = step_index.astype(jnp.float32)
    step_size = plan_sigma(position + 1.0) - plan_sigma(position)
    next_rows = (
        latent_f
        + step_size * velocity.astype(jnp.float32)
        + NOISE_LEVEL * jnp.sqrt(-step_size) * step_noise[0].astype(jnp.float32)
    )
    return (velocity[None], next_rows.astype(jnp.bfloat16)[None])


def solution(mesh):
    in_specs = (
        P("fsdp", "sp", None),
        P("fsdp", "sp", None),
        P(None, "fsdp", "sp"),
        P(None, "fsdp", None),
        P(None, None, "sp"),
        P("sp", "fsdp"),
        P("sp", None),
        P(None, "fsdp"),
        P(),
        P("fsdp"),
    )
    out_specs = (P("fsdp", "sp", None), P("fsdp", "sp", None))
    return jax.shard_map(
        per_device, mesh=mesh, in_specs=in_specs, out_specs=out_specs, check_vma=False
    )
```

```python
import jax
import jax.numpy as jnp
from jax import lax
from jax.sharding import PartitionSpec as P

HEAD_DIM = 128
NSTEP = 16
QUAD = 4


EPSILON = 1e-06
SHIFT_FACTOR = 5.0
NOISE_LEVEL = 0.7


def plan_sigma(position):
    ramp = 1.0 - position / NSTEP
    return SHIFT_FACTOR * ramp / (1.0 + (SHIFT_FACTOR - 1.0) * ramp)


def fsdp_index(z, y, x):
    return ((z % QUAD) * QUAD + y % QUAD) * QUAD + x % QUAD


Y_GROUPS = [[fsdp_index(z, y, x) for y in range(QUAD)] for z in range(QUAD) for x in range(QUAD)]
Z_GROUPS = [[fsdp_index(z, y, x) for z in range(QUAD)] for y in range(QUAD) for x in range(QUAD)]
X_GROUPS = [[fsdp_index(z, y, x) for x in range(QUAD)] for z in range(QUAD) for y in range(QUAD)]


def shift_fsdp(value, dy=0, dx=0):
    pairs = [
        (fsdp_index(z, y, x), fsdp_index(z, y + dy, x + dx))
        for z in range(QUAD)
        for y in range(QUAD)
        for x in range(QUAD)
    ]
    return lax.ppermute(value, "fsdp", pairs)


def shift_run(value, dz):
    pairs = [
        (z * 2 + core, ((z + dz) % QUAD) * 2 + core) for z in range(QUAD) for core in range(2)
    ]
    return lax.ppermute(value, "sp", pairs)


def place(buffer, block, axis, index):
    start = [jnp.int32(0)] * buffer.ndim
    start[axis] = index.astype(jnp.int32)
    return lax.dynamic_update_slice(buffer, jnp.expand_dims(block, axis), start)


def other_core(value):
    return lax.ppermute(value, "sp", [(i, i ^ 1) for i in range(2 * QUAD)])


def exchange(value, axis, groups):
    return lax.all_to_all(value, axis, 0, 0, axis_index_groups=groups, tiled=True)


def gather(value, axis, groups):
    return exchange(jnp.broadcast_to(value[None], (QUAD,) + value.shape), axis, groups)


def after(value, earlier):
    return value + earlier.ravel()[0] * 0


def per_device(
    latents,
    step_noise,
    base_qkv,
    down_qkv,
    up_query_key_value,
    base_out,
    down_out,
    up_out,
    modulation,
    timestep,
):
    y = lax.axis_index("fsdp") // QUAD % QUAD
    x = lax.axis_index("fsdp") % QUAD
    rows, width = latents.shape[1:]
    part = base_qkv.shape[1]
    head_cols = base_qkv.shape[2]
    heads_here = head_cols // HEAD_DIM
    seq_len = rows * 2 * QUAD
    slab = width // QUAD

    lowrank = jnp.einsum(
        "prk,pkc->prc", down_qkv, up_query_key_value, preferred_element_type=jnp.float32
    )
    merged_qkv = (base_qkv.astype(jnp.float32) + lowrank).astype(jnp.bfloat16)
    lowrank_out = jnp.einsum("rk,kc->cr", down_out, up_out, preferred_element_type=jnp.float32)
    merged_out = (base_out.T.astype(jnp.float32) + lowrank_out).astype(jnp.bfloat16)

    merged = jnp.concatenate([merged_qkv, merged_out[None]], axis=0)
    held = lax.all_gather(merged, "fsdp", axis_index_groups=Z_GROUPS, axis=0)

    weights = gather(held[:, :3], "fsdp", X_GROUPS).transpose(2, 1, 0, 3, 4)
    weights = weights.reshape(3, slab, head_cols)

    row = jnp.zeros((QUAD, QUAD, part, head_cols), jnp.bfloat16)
    for k in range(QUAD):
        block = held[:, 3] if k == 0 else shift_fsdp(held[:, 3], dy=k)
        row = place(row, block, 1, (y - k) % QUAD)
    out_rows = jnp.zeros((QUAD, QUAD, QUAD, part, head_cols), jnp.bfloat16)
    for k in range(QUAD):
        block = row if k == 0 else shift_fsdp(row, dx=k)
        out_rows = place(out_rows, block, 2, (x - k) % QUAD)
    out_rows = out_rows.reshape(width, head_cols)

    step_index = timestep[0]
    mod_rows = lax.dynamic_index_in_dim(modulation, step_index, 0, keepdims=False)
    latent_f = latents[0].astype(jnp.float32)
    mean_square = jnp.mean(latent_f * latent_f, axis=-1, keepdims=True)
    normalized_rows = (
        latent_f * lax.rsqrt(mean_square + EPSILON) * (1.0 + mod_rows[1]) + mod_rows[0]
    ).astype(jnp.bfloat16)
    slices = normalized_rows.reshape(rows, QUAD, QUAD, slab // QUAD).transpose(2, 0, 1, 3)
    mine = exchange(slices.reshape(QUAD, rows, slab), "fsdp", Y_GROUPS)
    mine = after(mine, held)
    run = jnp.stack([mine] + [shift_run(mine, k) for k in range(1, QUAD)], axis=1)
    both = jnp.stack([run, other_core(run)], axis=2)
    tokens = both.reshape(QUAD * seq_len, slab)

    partial = jnp.stack(
        [
            jnp.dot(tokens, weights[p], preferred_element_type=jnp.float32)
            .astype(jnp.bfloat16)
            .reshape(QUAD, seq_len, head_cols)
            for p in range(3)
        ],
        axis=1,
    )
    projected = exchange(partial, "fsdp", Y_GROUPS).astype(jnp.float32)
    projected = jnp.sum(projected, axis=0).astype(jnp.bfloat16)
    heads = projected.reshape(3, seq_len, heads_here, HEAD_DIM).transpose(0, 2, 1, 3)
    scores = jnp.einsum("hqe,hke->hqk", heads[0], heads[1], preferred_element_type=jnp.float32)
    attention_weights = jax.nn.softmax(scores * (1.0 / HEAD_DIM**0.5), axis=-1).astype(jnp.bfloat16)
    attended = jnp.einsum(
        "hqk,hke->qhe", attention_weights, heads[2], preferred_element_type=jnp.float32
    ).astype(jnp.bfloat16)
    attended = attended.reshape(seq_len, head_cols)

    by_core = attended.reshape(QUAD, 2, rows, head_cols)

    def project_out(flip):
        return lax.dot_general(
            by_core[:, flip].reshape(QUAD * rows, head_cols),
            out_rows,
            (((1,), (1,)), ((), ())),
            preferred_element_type=jnp.float32,
        )

    theirs = other_core(project_out(1).astype(jnp.bfloat16)).astype(jnp.float32)
    pair = (project_out(0) + theirs).reshape(QUAD, rows, width)
    block_out = pair[0]
    for k in range(1, QUAD):
        block_out = block_out + shift_run(pair[k].astype(jnp.bfloat16), -k).astype(jnp.float32)

    velocity = ((1.0 + mod_rows[2]) * block_out).astype(jnp.bfloat16)
    position = step_index.astype(jnp.float32)
    step_size = plan_sigma(position + 1.0) - plan_sigma(position)
    next_rows = (
        latent_f
        + step_size * velocity.astype(jnp.float32)
        + NOISE_LEVEL * jnp.sqrt(-step_size) * step_noise[0].astype(jnp.float32)
    )
    return (velocity[None], next_rows.astype(jnp.bfloat16)[None])


def solution(mesh):
    in_specs = (
        P("fsdp", "sp", None),
        P("fsdp", "sp", None),
        P(None, "fsdp", "sp"),
        P(None, "fsdp", None),
        P(None, None, "sp"),
        P("sp", "fsdp"),
        P("sp", None),
        P(None, "fsdp"),
        P(),
        P("fsdp"),
    )
    out_specs = (P("fsdp", "sp", None), P("fsdp", "sp", None))
    return jax.shard_map(
        per_device, mesh=mesh, in_specs=in_specs, out_specs=out_specs, check_vma=False
    )
```

```python
import jax
import jax.numpy as jnp
from jax import lax
from jax.experimental import pallas as pl
from jax.experimental.pallas import tpu as pltpu
from jax.sharding import PartitionSpec as P

HEAD_DIM = 128
NSTEP = 16
QUAD = 4


EPSILON = 1e-06
SHIFT_FACTOR = 5.0
NOISE_LEVEL = 0.7


def plan_sigma(position):
    ramp = 1.0 - position / NSTEP
    return SHIFT_FACTOR * ramp / (1.0 + (SHIFT_FACTOR - 1.0) * ramp)


def fsdp_index(z, y, x):
    return ((z % QUAD) * QUAD + y % QUAD) * QUAD + x % QUAD


Y_GROUPS = [[fsdp_index(z, y, x) for y in range(QUAD)] for z in range(QUAD) for x in range(QUAD)]
Z_GROUPS = [[fsdp_index(z, y, x) for z in range(QUAD)] for y in range(QUAD) for x in range(QUAD)]
X_GROUPS = [[fsdp_index(z, y, x) for x in range(QUAD)] for z in range(QUAD) for y in range(QUAD)]


def shift_fsdp(value, dy=0, dx=0):
    pairs = [
        (fsdp_index(z, y, x), fsdp_index(z, y + dy, x + dx))
        for z in range(QUAD)
        for y in range(QUAD)
        for x in range(QUAD)
    ]
    return lax.ppermute(value, "fsdp", pairs)


def shift_run(value, dz):
    pairs = [
        (z * 2 + core, ((z + dz) % QUAD) * 2 + core) for z in range(QUAD) for core in range(2)
    ]
    return lax.ppermute(value, "sp", pairs)


def other_core(value):
    return lax.ppermute(value, "sp", [(i, i ^ 1) for i in range(2 * QUAD)])


def exchange(value, axis, groups):
    return lax.all_to_all(value, axis, 0, 0, axis_index_groups=groups, tiled=True)


def gather(value, axis, groups):
    return exchange(jnp.broadcast_to(value[None], (QUAD,) + value.shape), axis, groups)


def prepare_kernel(
    step_ref,
    latents_ref,
    modulation_ref,
    base_qkv_ref,
    down_qkv_ref,
    up_qkv_ref,
    base_out_ref,
    down_out_ref,
    up_out_ref,
    slices_ref,
    merged_ref,
):
    for p in range(3):
        lowrank = jnp.dot(down_qkv_ref[p], up_qkv_ref[p], preferred_element_type=jnp.float32)
        merged_ref[p] = (base_qkv_ref[p].astype(jnp.float32) + lowrank).astype(jnp.bfloat16)
    lowrank = jnp.dot(up_out_ref[...], down_out_ref[...], preferred_element_type=jnp.float32)
    merged_ref[3] = (base_out_ref[...].astype(jnp.float32) + lowrank).astype(jnp.bfloat16)

    step = step_ref[0]
    shift = modulation_ref[0, pl.ds(step, 1), :]
    scale = modulation_ref[1, pl.ds(step, 1), :]
    latent = latents_ref[...].astype(jnp.float32)
    mean_square = jnp.mean(latent * latent, axis=-1, keepdims=True)
    normed = latent * lax.rsqrt(mean_square + EPSILON) * (1.0 + scale) + shift
    slab = normed.shape[1] // QUAD
    piece = slab // QUAD
    x = lax.axis_index("fsdp") % QUAD
    for y in range(QUAD):
        blocks = [
            normed[:, z * slab + y * piece : z * slab + (y + 1) * piece] for z in range(QUAD)
        ]
        mine = jnp.concatenate(blocks, axis=1)
        for step in range(1, QUAD):
            cut = step * piece // QUAD
            turned = [part for block in blocks for part in (block[:, cut:], block[:, :cut])]
            mine = jnp.where(x == step, jnp.concatenate(turned, axis=1), mine)
        slices_ref[y] = mine.astype(jnp.bfloat16)


def attend_kernel(own_ref, first_ref, second_ref, third_ref, weights_ref, mine_ref, theirs_ref):
    projected = own_ref[...].astype(jnp.float32)
    for ref in (first_ref, second_ref, third_ref):
        projected = projected + ref[...].astype(jnp.float32)
    projected = projected.astype(jnp.bfloat16)
    columns = projected.shape[1] // 3
    heads = []
    for h in range(columns // HEAD_DIM):
        queries, keys, values = (
            projected[:, p * columns + h * HEAD_DIM : p * columns + (h + 1) * HEAD_DIM]
            for p in range(3)
        )
        scores = lax.dot_general(
            queries, keys, (((1,), (1,)), ((), ())), preferred_element_type=jnp.float32
        ) * (1.0 / HEAD_DIM**0.5)
        weights = jnp.exp(scores - jnp.max(scores, axis=-1, keepdims=True))
        weights = weights / jnp.sum(weights, axis=-1, keepdims=True)
        heads.append(
            jnp.dot(
                weights.astype(jnp.bfloat16), values, preferred_element_type=jnp.float32
            ).astype(jnp.bfloat16)
        )
    attended = jnp.concatenate(heads, axis=1)
    half, slab = mine_ref.shape[0], weights_ref.shape[1]
    for k in range(QUAD):
        out = lax.dot_general(
            attended, weights_ref[k], (((1,), (1,)), ((), ())), preferred_element_type=jnp.float32
        ).astype(jnp.bfloat16)
        mine_ref[:, k * slab : (k + 1) * slab] = out[:half]
        theirs_ref[:, k * slab : (k + 1) * slab] = out[half:]


def finish_kernel(
    step_ref,
    own_ref,
    first_ref,
    second_ref,
    third_ref,
    latents_ref,
    noise_ref,
    modulation_ref,
    velocity_ref,
    next_ref,
):
    step = step_ref[0]
    block_out = own_ref[...].astype(jnp.float32)
    for ref in (first_ref, second_ref, third_ref):
        block_out = block_out + ref[...].astype(jnp.float32)
    piece = block_out.shape[1] // QUAD**3
    starts = [
        ((x * QUAD + y) * QUAD + z) * piece
        for z in range(QUAD)
        for y in range(QUAD)
        for x in range(QUAD)
    ]
    ordered = jnp.concatenate([block_out[:, i : i + piece] for i in starts], axis=1)
    gate = modulation_ref[2, pl.ds(step, 1), :]
    velocity = ((1.0 + gate) * ordered).astype(jnp.bfloat16)
    velocity_ref[...] = velocity
    position = jnp.full((1, 1), step, jnp.int32).astype(jnp.float32)
    step_size = plan_sigma(position + 1.0) - plan_sigma(position)
    next_ref[...] = (
        latents_ref[...].astype(jnp.float32)
        + step_size * velocity.astype(jnp.float32)
        + NOISE_LEVEL * jnp.sqrt(-step_size) * noise_ref[...].astype(jnp.float32)
    ).astype(jnp.bfloat16)


def whole(shape):
    return pl.BlockSpec(shape, lambda i: (0,) * len(shape))


def call(kernel, out_shapes, *operands, scalars=0, mebibytes=40):
    smem = pl.BlockSpec(memory_space=pltpu.SMEM)
    return pl.pallas_call(
        kernel,
        grid=(1,),
        out_shape=out_shapes,
        in_specs=[smem] * scalars + [whole(x.shape) for x in operands[scalars:]],
        out_specs=jax.tree.map(lambda x: whole(x.shape), out_shapes),
        compiler_params=pltpu.CompilerParams(vmem_limit_bytes=mebibytes * 2**20),
    )(*operands)


def per_device(
    latents,
    step_noise,
    base_qkv,
    down_qkv,
    up_query_key_value,
    base_out,
    down_out,
    up_out,
    modulation,
    timestep,
):
    y = lax.axis_index("fsdp") // QUAD % QUAD
    rows, width = latents.shape[1:]
    part = base_qkv.shape[1]
    head_cols = base_qkv.shape[2]
    seq_len = rows * 2 * QUAD
    slab = width // QUAD

    slices, merged = call(
        prepare_kernel,
        (
            jax.ShapeDtypeStruct((QUAD, rows, slab), jnp.bfloat16),
            jax.ShapeDtypeStruct((4, part, head_cols), jnp.bfloat16),
        ),
        timestep,
        latents[0],
        modulation.transpose(1, 0, 2),
        base_qkv,
        down_qkv,
        up_query_key_value,
        base_out.T,
        down_out.T,
        up_out.T,
        scalars=1,
        mebibytes=60,
    )

    mine = exchange(slices, "fsdp", Y_GROUPS)
    mine = jnp.concatenate([mine, mine], axis=0)
    mine = lax.rev(lax.dynamic_slice_in_dim(mine, y + 1, QUAD, 0), (0,))

    held = lax.all_gather(merged, "fsdp", axis_index_groups=Z_GROUPS, axis=0)

    moving = held[:, :3]
    blocks = [moving] + [shift_fsdp(moving, dx=-k) for k in range(1, QUAD)]
    weights = jnp.stack(blocks, axis=1).transpose(0, 1, 3, 2, 4).reshape(slab, 3 * head_cols)

    out_rows = gather(held[:, 3].reshape(QUAD * part, head_cols), "fsdp", Y_GROUPS)
    out_rows = gather(out_rows.reshape(slab, head_cols), "fsdp", X_GROUPS)
    mine, held = lax.optimization_barrier((mine, held))

    run = jnp.stack([mine] + [shift_run(mine, k) for k in range(1, QUAD)], axis=1)
    tokens = jnp.stack([run, other_core(run)], axis=1).reshape(QUAD * seq_len, slab)

    partial = jnp.dot(tokens, weights, preferred_element_type=jnp.float32).astype(jnp.bfloat16)
    partial = partial.reshape(QUAD, seq_len, 3 * head_cols)
    parts = [partial[0]] + [shift_fsdp(partial[k], dy=-k) for k in (2, 1, 3)]

    half = seq_len // 2
    ours, theirs = call(
        attend_kernel,
        (jax.ShapeDtypeStruct((half, width), jnp.bfloat16),) * 2,
        *parts,
        out_rows,
    )
    pair = ours.astype(jnp.float32) + other_core(theirs).astype(jnp.float32)
    pair = pair.astype(jnp.bfloat16).reshape(QUAD, rows, width)
    returned = [pair[0]] + [shift_run(pair[k], -k) for k in (2, 1, 3)]
    velocity, next_rows = call(
        finish_kernel,
        (jax.ShapeDtypeStruct((rows, width), jnp.bfloat16),) * 2,
        timestep,
        *returned,
        latents[0],
        step_noise[0],
        modulation.transpose(1, 0, 2),
        scalars=1,
    )
    return (velocity[None], next_rows[None])


def solution(mesh):
    in_specs = (
        P("fsdp", "sp", None),
        P("fsdp", "sp", None),
        P(None, "fsdp", "sp"),
        P(None, "fsdp", None),
        P(None, None, "sp"),
        P("sp", "fsdp"),
        P("sp", None),
        P(None, "fsdp"),
        P(),
        P("fsdp"),
    )
    out_specs = (P("fsdp", "sp", None), P("fsdp", "sp", None))
    return jax.shard_map(
        per_device, mesh=mesh, in_specs=in_specs, out_specs=out_specs, check_vma=False
    )
```

```python
import jax
import jax.numpy as jnp
from jax import lax
from jax.experimental import pallas as pl
from jax.experimental.pallas import tpu as pltpu
from jax.sharding import PartitionSpec as P

HEAD_DIM = 128
NSTEP = 16
QUAD = 4


EPSILON = 1e-06
SHIFT_FACTOR = 5.0
NOISE_LEVEL = 0.7


def plan_sigma(position):
    ramp = 1.0 - position / NSTEP
    return SHIFT_FACTOR * ramp / (1.0 + (SHIFT_FACTOR - 1.0) * ramp)


def fsdp_index(z, y, x):
    return ((z % QUAD) * QUAD + y % QUAD) * QUAD + x % QUAD


Y_GROUPS = [[fsdp_index(z, y, x) for y in range(QUAD)] for z in range(QUAD) for x in range(QUAD)]
Z_GROUPS = [[fsdp_index(z, y, x) for z in range(QUAD)] for y in range(QUAD) for x in range(QUAD)]
X_GROUPS = [[fsdp_index(z, y, x) for x in range(QUAD)] for z in range(QUAD) for y in range(QUAD)]


def shift_fsdp(value, dy=0, dx=0):
    pairs = [
        (fsdp_index(z, y, x), fsdp_index(z, y + dy, x + dx))
        for z in range(QUAD)
        for y in range(QUAD)
        for x in range(QUAD)
    ]
    return lax.ppermute(value, "fsdp", pairs)


def shift_run(value, dz):
    pairs = [
        (z * 2 + core, ((z + dz) % QUAD) * 2 + core) for z in range(QUAD) for core in range(2)
    ]
    return lax.ppermute(value, "sp", pairs)


def other_core(value):
    return lax.ppermute(value, "sp", [(i, i ^ 1) for i in range(2 * QUAD)])


def exchange(value, axis, groups):
    return lax.all_to_all(value, axis, 0, 0, axis_index_groups=groups, tiled=True)


def gather(value, axis, groups):
    return exchange(jnp.broadcast_to(value[None], (QUAD,) + value.shape), axis, groups)


def prepare_kernel(
    step_ref,
    latents_ref,
    modulation_ref,
    base_qkv_ref,
    down_qkv_ref,
    up_qkv_ref,
    base_out_ref,
    down_out_ref,
    up_out_ref,
    slices_ref,
    merged_ref,
    by_x,
):
    for p in range(3):
        lowrank = jnp.dot(down_qkv_ref[p], up_qkv_ref[p], preferred_element_type=jnp.float32)
        merged_ref[p] = (base_qkv_ref[p].astype(jnp.float32) + lowrank).astype(jnp.bfloat16)
    lowrank = jnp.dot(up_out_ref[...], down_out_ref[...], preferred_element_type=jnp.float32)
    merged_ref[3] = (base_out_ref[...].astype(jnp.float32) + lowrank).astype(jnp.bfloat16)

    step = step_ref[0]
    shift = modulation_ref[0, pl.ds(step, 1), :]
    scale = modulation_ref[1, pl.ds(step, 1), :]
    latent = latents_ref[...].astype(jnp.float32)
    mean_square = jnp.mean(latent * latent, axis=-1, keepdims=True)
    normed = latent * lax.rsqrt(mean_square + EPSILON) * (1.0 + scale) + shift
    slab = normed.shape[1] // QUAD
    piece = slab // QUAD
    x_here = lax.axis_index("fsdp") % QUAD
    part = piece // QUAD
    for y in range(QUAD):
        for x in range(QUAD):
            starts = [z * slab + y * piece + x * part for z in range(QUAD)]
            by_x[x] = jnp.concatenate([normed[:, i : i + part] for i in starts], axis=1)
        turned = [by_x[lax.rem(x_here + k, QUAD)] for k in range(QUAD)]
        slices_ref[y] = jnp.concatenate(turned, axis=1).astype(jnp.bfloat16)


def attend_kernel(projected_ref, weights_ref, mine_ref, theirs_ref):
    projected = projected_ref[...]
    columns = projected.shape[1] // 3
    heads = []
    for h in range(columns // HEAD_DIM):
        queries, keys, values = (
            projected[:, p * columns + h * HEAD_DIM : p * columns + (h + 1) * HEAD_DIM]
            for p in range(3)
        )
        scores = lax.dot_general(
            queries, keys, (((1,), (1,)), ((), ())), preferred_element_type=jnp.float32
        ) * (1.0 / HEAD_DIM**0.5)
        weights = jnp.exp(scores - jnp.max(scores, axis=-1, keepdims=True))
        weights = weights / jnp.sum(weights, axis=-1, keepdims=True)
        heads.append(
            jnp.dot(
                weights.astype(jnp.bfloat16), values, preferred_element_type=jnp.float32
            ).astype(jnp.bfloat16)
        )
    attended = jnp.concatenate(heads, axis=1)
    half, slab = mine_ref.shape[0], weights_ref.shape[1]
    for k in range(QUAD):
        out = lax.dot_general(
            attended, weights_ref[k], (((1,), (1,)), ((), ())), preferred_element_type=jnp.float32
        ).astype(jnp.bfloat16)
        mine_ref[:, k * slab : (k + 1) * slab] = out[:half]
        theirs_ref[:, k * slab : (k + 1) * slab] = out[half:]


def finish_kernel(
    step_ref,
    own_ref,
    first_ref,
    second_ref,
    third_ref,
    latents_ref,
    noise_ref,
    modulation_ref,
    velocity_ref,
    next_ref,
):
    step = step_ref[0]
    block_out = own_ref[...].astype(jnp.float32)
    for ref in (first_ref, second_ref, third_ref):
        block_out = block_out + ref[...].astype(jnp.float32)
    piece = block_out.shape[1] // QUAD**3
    starts = [
        ((x * QUAD + y) * QUAD + z) * piece
        for z in range(QUAD)
        for y in range(QUAD)
        for x in range(QUAD)
    ]
    ordered = jnp.concatenate([block_out[:, i : i + piece] for i in starts], axis=1)
    gate = modulation_ref[2, pl.ds(step, 1), :]
    velocity = ((1.0 + gate) * ordered).astype(jnp.bfloat16)
    velocity_ref[...] = velocity
    position = jnp.full((1, 1), step, jnp.int32).astype(jnp.float32)
    step_size = plan_sigma(position + 1.0) - plan_sigma(position)
    next_ref[...] = (
        latents_ref[...].astype(jnp.float32)
        + step_size * velocity.astype(jnp.float32)
        + NOISE_LEVEL * jnp.sqrt(-step_size) * noise_ref[...].astype(jnp.float32)
    ).astype(jnp.bfloat16)


def hold_kernel(*refs):
    pass


def hold(values, earlier):
    held = pl.BlockSpec(memory_space=pl.ANY)
    return pl.pallas_call(
        hold_kernel,
        out_shape=[jax.ShapeDtypeStruct(x.shape, x.dtype) for x in values],
        in_specs=[held] * (len(values) + 1),
        out_specs=[held] * len(values),
        input_output_aliases={i: i for i in range(len(values))},
        cost_estimate=pl.CostEstimate(flops=4 * 10**9, bytes_accessed=0, transcendentals=0),
    )(*values, earlier)


def whole(shape):
    return pl.BlockSpec(shape, lambda i: (0,) * len(shape))


def call(kernel, out_shapes, *operands, scalars=0, mebibytes=40, scratch=()):
    smem = pl.BlockSpec(memory_space=pltpu.SMEM)
    return pl.pallas_call(
        kernel,
        grid=(1,),
        out_shape=out_shapes,
        in_specs=[smem] * scalars + [whole(x.shape) for x in operands[scalars:]],
        out_specs=jax.tree.map(lambda x: whole(x.shape), out_shapes),
        scratch_shapes=scratch,
        compiler_params=pltpu.CompilerParams(vmem_limit_bytes=mebibytes * 2**20),
    )(*operands)


def per_device(
    latents,
    step_noise,
    base_qkv,
    down_qkv,
    up_query_key_value,
    base_out,
    down_out,
    up_out,
    modulation,
    timestep,
):
    y = lax.axis_index("fsdp") // QUAD % QUAD
    rows, width = latents.shape[1:]
    part = base_qkv.shape[1]
    head_cols = base_qkv.shape[2]
    seq_len = rows * 2 * QUAD
    slab = width // QUAD

    slices, merged = call(
        prepare_kernel,
        (
            jax.ShapeDtypeStruct((QUAD, rows, slab), jnp.bfloat16),
            jax.ShapeDtypeStruct((4, part, head_cols), jnp.bfloat16),
        ),
        timestep,
        latents[0],
        modulation.transpose(1, 0, 2),
        base_qkv,
        down_qkv,
        up_query_key_value,
        base_out.T,
        down_out.T,
        up_out.T,
        scalars=1,
        mebibytes=60,
        scratch=[pltpu.VMEM((QUAD, rows, slab // QUAD), jnp.float32)],
    )

    mine = exchange(slices, "fsdp", Y_GROUPS)
    mine = jnp.concatenate([mine, mine], axis=0)
    mine = lax.rev(lax.dynamic_slice_in_dim(mine, y + 1, QUAD, 0), (0,))

    held = lax.all_gather(merged, "fsdp", axis_index_groups=Z_GROUPS, axis=0)

    moving = held[:, :3].transpose(0, 2, 1, 3).reshape(QUAD * part, 3 * head_cols)
    own_rows = held[:, 3].reshape(QUAD * part, head_cols)
    mine, moving = lax.optimization_barrier((mine, moving))
    blocks = [moving] + [shift_fsdp(moving, dx=-k) for k in range(1, QUAD)]

    run = jnp.stack([mine] + [shift_run(mine, k) for k in range(1, QUAD)], axis=1)

    out_rows = gather(own_rows, "fsdp", Y_GROUPS).reshape(slab, head_cols)
    copies = jnp.broadcast_to(out_rows[None], (QUAD, slab, head_cols))
    blocks = blocks[:1] + list(hold(blocks[1:], out_rows))
    out_rows = exchange(copies, "fsdp", X_GROUPS)
    weights = jnp.concatenate(blocks, axis=0)

    tokens = jnp.stack([run, other_core(run)], axis=1).reshape(QUAD * seq_len, slab)

    partial = jnp.dot(tokens, weights, preferred_element_type=jnp.float32).astype(jnp.bfloat16)
    partial = partial.reshape(QUAD, seq_len, 3 * head_cols)
    projected = partial[0].astype(jnp.float32)
    for k in (2, 1, 3):
        projected = projected + shift_fsdp(partial[k], dy=-k).astype(jnp.float32)
    projected = projected.astype(jnp.bfloat16)

    half = seq_len // 2
    ours, theirs = call(
        attend_kernel,
        (jax.ShapeDtypeStruct((half, width), jnp.bfloat16),) * 2,
        projected,
        out_rows,
    )
    pair = ours.astype(jnp.float32) + other_core(theirs).astype(jnp.float32)
    pair = pair.astype(jnp.bfloat16).reshape(QUAD, rows, width)
    returned = [pair[0]] + [shift_run(pair[k], -k) for k in (2, 1, 3)]
    velocity, next_rows = call(
        finish_kernel,
        (jax.ShapeDtypeStruct((rows, width), jnp.bfloat16),) * 2,
        timestep,
        *returned,
        latents[0],
        step_noise[0],
        modulation.transpose(1, 0, 2),
        scalars=1,
        mebibytes=40,
    )
    return (velocity[None], next_rows[None])


def solution(mesh):
    in_specs = (
        P("fsdp", "sp", None),
        P("fsdp", "sp", None),
        P(None, "fsdp", "sp"),
        P(None, "fsdp", None),
        P(None, None, "sp"),
        P("sp", "fsdp"),
        P("sp", None),
        P(None, "fsdp"),
        P(),
        P("fsdp"),
    )
    out_specs = (P("fsdp", "sp", None), P("fsdp", "sp", None))
    return jax.shard_map(
        per_device, mesh=mesh, in_specs=in_specs, out_specs=out_specs, check_vma=False
    )
```

```python
import jax
import jax.numpy as jnp
from jax import lax
from jax.experimental import pallas as pl
from jax.experimental.pallas import tpu as pltpu
from jax.sharding import PartitionSpec as P

HEAD_DIM = 128
NSTEP = 16
QUAD = 4


EPSILON = 1e-06
SHIFT_FACTOR = 5.0
NOISE_LEVEL = 0.7


def plan_sigma(position):
    ramp = 1.0 - position / NSTEP
    return SHIFT_FACTOR * ramp / (1.0 + (SHIFT_FACTOR - 1.0) * ramp)


def fsdp_index(z, y, x):
    return ((z % QUAD) * QUAD + y % QUAD) * QUAD + x % QUAD


Y_GROUPS = [[fsdp_index(z, y, x) for y in range(QUAD)] for z in range(QUAD) for x in range(QUAD)]
Z_GROUPS = [[fsdp_index(z, y, x) for z in range(QUAD)] for y in range(QUAD) for x in range(QUAD)]
X_GROUPS = [[fsdp_index(z, y, x) for x in range(QUAD)] for z in range(QUAD) for y in range(QUAD)]


def shift_fsdp(value, dy=0, dx=0):
    pairs = [
        (fsdp_index(z, y, x), fsdp_index(z, y + dy, x + dx))
        for z in range(QUAD)
        for y in range(QUAD)
        for x in range(QUAD)
    ]
    return lax.ppermute(value, "fsdp", pairs)


def shift_run(value, dz):
    pairs = [
        (z * 2 + core, ((z + dz) % QUAD) * 2 + core) for z in range(QUAD) for core in range(2)
    ]
    return lax.ppermute(value, "sp", pairs)


def other_core(value):
    return lax.ppermute(value, "sp", [(i, i ^ 1) for i in range(2 * QUAD)])


def exchange(value, axis, groups):
    return lax.all_to_all(value, axis, 0, 0, axis_index_groups=groups, tiled=True)


def gather(value, axis, groups):
    return exchange(jnp.broadcast_to(value[None], (QUAD,) + value.shape), axis, groups)


def prepare_kernel(
    step_ref,
    latents_ref,
    modulation_ref,
    base_qkv_ref,
    down_qkv_ref,
    up_qkv_ref,
    base_out_ref,
    down_out_ref,
    up_out_ref,
    slices_ref,
    merged_ref,
    by_x,
):
    for p in range(3):
        lowrank = jnp.dot(down_qkv_ref[p], up_qkv_ref[p], preferred_element_type=jnp.float32)
        merged_ref[p] = (base_qkv_ref[p].astype(jnp.float32) + lowrank).astype(jnp.bfloat16)
    lowrank = jnp.dot(up_out_ref[...], down_out_ref[...], preferred_element_type=jnp.float32)
    merged_ref[3] = (base_out_ref[...].astype(jnp.float32) + lowrank).astype(jnp.bfloat16)

    here = lax.broadcasted_iota(jnp.int32, (NSTEP, 1), 0) == step_ref[...]
    shift = jnp.sum(jnp.where(here, modulation_ref[0], 0.0), axis=0, keepdims=True)
    scale = jnp.sum(jnp.where(here, modulation_ref[1], 0.0), axis=0, keepdims=True)
    latent = latents_ref[...].astype(jnp.float32)
    mean_square = jnp.mean(latent * latent, axis=-1, keepdims=True)
    normed = latent * lax.rsqrt(mean_square + EPSILON) * (1.0 + scale) + shift
    slab = normed.shape[1] // QUAD
    piece = slab // QUAD
    x_here = lax.axis_index("fsdp") % QUAD
    part = piece // QUAD
    for y in range(QUAD):
        for x in range(QUAD):
            starts = [z * slab + y * piece + x * part for z in range(QUAD)]
            by_x[x] = jnp.concatenate([normed[:, i : i + part] for i in starts], axis=1)
        turned = [by_x[lax.rem(x_here + k, QUAD)] for k in range(QUAD)]
        slices_ref[y] = jnp.concatenate(turned, axis=1).astype(jnp.bfloat16)


def attend_kernel(projected_ref, weights_ref, mine_ref, theirs_ref):
    projected = projected_ref[...]
    columns = projected.shape[1] // 3
    heads = []
    for h in range(columns // HEAD_DIM):
        queries, keys, values = (
            projected[:, p * columns + h * HEAD_DIM : p * columns + (h + 1) * HEAD_DIM]
            for p in range(3)
        )
        scores = lax.dot_general(
            queries, keys, (((1,), (1,)), ((), ())), preferred_element_type=jnp.float32
        ) * (1.0 / HEAD_DIM**0.5)
        weights = jnp.exp(scores - jnp.max(scores, axis=-1, keepdims=True))
        weights = weights / jnp.sum(weights, axis=-1, keepdims=True)
        heads.append(
            jnp.dot(
                weights.astype(jnp.bfloat16), values, preferred_element_type=jnp.float32
            ).astype(jnp.bfloat16)
        )
    attended = jnp.concatenate(heads, axis=1)
    half, slab = mine_ref.shape[0], weights_ref.shape[1]
    for k in range(QUAD):
        out = lax.dot_general(
            attended, weights_ref[k], (((1,), (1,)), ((), ())), preferred_element_type=jnp.float32
        ).astype(jnp.bfloat16)
        mine_ref[:, k * slab : (k + 1) * slab] = out[:half]
        theirs_ref[:, k * slab : (k + 1) * slab] = out[half:]


def finish_kernel(
    step_ref,
    own_ref,
    first_ref,
    second_ref,
    third_ref,
    latents_ref,
    noise_ref,
    modulation_ref,
    velocity_ref,
    next_ref,
):
    step = step_ref[0]
    block_out = own_ref[...].astype(jnp.float32)
    for ref in (first_ref, second_ref, third_ref):
        block_out = block_out + ref[...].astype(jnp.float32)
    piece = block_out.shape[1] // QUAD**3
    starts = [
        ((x * QUAD + y) * QUAD + z) * piece
        for z in range(QUAD)
        for y in range(QUAD)
        for x in range(QUAD)
    ]
    ordered = jnp.concatenate([block_out[:, i : i + piece] for i in starts], axis=1)
    gate = modulation_ref[2, pl.ds(step, 1), :]
    velocity = ((1.0 + gate) * ordered).astype(jnp.bfloat16)
    velocity_ref[...] = velocity
    position = jnp.full((1, 1), step, jnp.int32).astype(jnp.float32)
    step_size = plan_sigma(position + 1.0) - plan_sigma(position)
    next_ref[...] = (
        latents_ref[...].astype(jnp.float32)
        + step_size * velocity.astype(jnp.float32)
        + NOISE_LEVEL * jnp.sqrt(-step_size) * noise_ref[...].astype(jnp.float32)
    ).astype(jnp.bfloat16)


def hold_kernel(*refs):
    pass


def hold(values, earlier):
    held = pl.BlockSpec(memory_space=pl.ANY)
    return pl.pallas_call(
        hold_kernel,
        out_shape=[jax.ShapeDtypeStruct(x.shape, x.dtype) for x in values],
        in_specs=[held] * (len(values) + 1),
        out_specs=[held] * len(values),
        input_output_aliases={i: i for i in range(len(values))},
        cost_estimate=pl.CostEstimate(flops=4 * 10**9, bytes_accessed=0, transcendentals=0),
    )(*values, earlier)


def whole(shape):
    return pl.BlockSpec(shape, lambda i: (0,) * len(shape))


def call(kernel, out_shapes, *operands, scalars=0, mebibytes=40, scratch=()):
    smem = pl.BlockSpec(memory_space=pltpu.SMEM)
    return pl.pallas_call(
        kernel,
        grid=(1,),
        out_shape=out_shapes,
        in_specs=[smem] * scalars + [whole(x.shape) for x in operands[scalars:]],
        out_specs=jax.tree.map(lambda x: whole(x.shape), out_shapes),
        scratch_shapes=scratch,
        compiler_params=pltpu.CompilerParams(vmem_limit_bytes=mebibytes * 2**20),
    )(*operands)


def per_device(
    latents,
    step_noise,
    base_qkv,
    down_qkv,
    up_query_key_value,
    base_out,
    down_out,
    up_out,
    modulation,
    timestep,
):
    y = lax.axis_index("fsdp") // QUAD % QUAD
    rows, width = latents.shape[1:]
    part = base_qkv.shape[1]
    head_cols = base_qkv.shape[2]
    seq_len = rows * 2 * QUAD
    slab = width // QUAD

    slices, merged = call(
        prepare_kernel,
        (
            jax.ShapeDtypeStruct((QUAD, rows, slab), jnp.bfloat16),
            jax.ShapeDtypeStruct((4, part, head_cols), jnp.bfloat16),
        ),
        timestep.reshape(1, 1),
        latents[0],
        modulation.transpose(1, 0, 2),
        base_qkv,
        down_qkv,
        up_query_key_value,
        base_out.T,
        down_out.T,
        up_out.T,
        mebibytes=60,
        scratch=[pltpu.VMEM((QUAD, rows, slab // QUAD), jnp.float32)],
    )

    mine = exchange(slices, "fsdp", Y_GROUPS)
    mine = jnp.concatenate([mine, mine], axis=0)
    mine = lax.rev(lax.dynamic_slice_in_dim(mine, y + 1, QUAD, 0), (0,))

    held = lax.all_gather(merged, "fsdp", axis_index_groups=Z_GROUPS, axis=0)

    moving = held[:, :3].transpose(0, 2, 1, 3).reshape(QUAD * part, 3 * head_cols)
    own_rows = held[:, 3].reshape(QUAD * part, head_cols)
    mine, held = lax.optimization_barrier((mine, held))
    blocks = [moving] + [shift_fsdp(moving, dx=-k) for k in range(1, QUAD)]

    run = jnp.stack([mine] + [shift_run(mine, k) for k in range(1, QUAD)], axis=1)

    out_rows = gather(own_rows, "fsdp", Y_GROUPS).reshape(slab, head_cols)
    copies = jnp.broadcast_to(out_rows[None], (QUAD, slab, head_cols))
    blocks = blocks[:1] + list(hold(blocks[1:], out_rows))
    out_rows = exchange(copies, "fsdp", X_GROUPS)
    weights = jnp.concatenate(blocks, axis=0)

    tokens = jnp.stack([run, other_core(run)], axis=1).reshape(QUAD * seq_len, slab)

    partial = jnp.dot(tokens, weights, preferred_element_type=jnp.float32).astype(jnp.bfloat16)
    partial = partial.reshape(QUAD, seq_len, 3 * head_cols)
    projected = partial[0].astype(jnp.float32)
    for k in (2, 1, 3):
        projected = projected + shift_fsdp(partial[k], dy=-k).astype(jnp.float32)
    projected = projected.astype(jnp.bfloat16)

    half = seq_len // 2
    ours, theirs = call(
        attend_kernel,
        (jax.ShapeDtypeStruct((half, width), jnp.bfloat16),) * 2,
        projected,
        out_rows,
    )
    pair = ours.astype(jnp.float32) + other_core(theirs).astype(jnp.float32)
    pair = pair.astype(jnp.bfloat16).reshape(QUAD, rows, width)
    returned = [pair[0]] + [shift_run(pair[k], -k) for k in (2, 1, 3)]
    velocity, next_rows = call(
        finish_kernel,
        (jax.ShapeDtypeStruct((rows, width), jnp.bfloat16),) * 2,
        timestep,
        *returned,
        latents[0],
        step_noise[0],
        modulation.transpose(1, 0, 2),
        scalars=1,
        mebibytes=40,
    )
    return (velocity[None], next_rows[None])


def solution(mesh):
    in_specs = (
        P("fsdp", "sp", None),
        P("fsdp", "sp", None),
        P(None, "fsdp", "sp"),
        P(None, "fsdp", None),
        P(None, None, "sp"),
        P("sp", "fsdp"),
        P("sp", None),
        P(None, "fsdp"),
        P(),
        P("fsdp"),
    )
    out_specs = (P("fsdp", "sp", None), P("fsdp", "sp", None))
    return jax.shard_map(
        per_device, mesh=mesh, in_specs=in_specs, out_specs=out_specs, check_vma=False
    )
```

```python
import jax
import jax.numpy as jnp
from jax import lax
from jax.experimental import pallas as pl
from jax.experimental.pallas import tpu as pltpu
from jax.sharding import PartitionSpec as P

HEAD_DIM = 128
NSTEP = 16
QUAD = 4


EPSILON = 1e-06
SHIFT_FACTOR = 5.0
NOISE_LEVEL = 0.7


def plan_sigma(position):
    ramp = 1.0 - position / NSTEP
    return SHIFT_FACTOR * ramp / (1.0 + (SHIFT_FACTOR - 1.0) * ramp)


def fsdp_index(z, y, x):
    return ((z % QUAD) * QUAD + y % QUAD) * QUAD + x % QUAD


Y_GROUPS = [[fsdp_index(z, y, x) for y in range(QUAD)] for z in range(QUAD) for x in range(QUAD)]
Z_GROUPS = [[fsdp_index(z, y, x) for z in range(QUAD)] for y in range(QUAD) for x in range(QUAD)]
X_GROUPS = [[fsdp_index(z, y, x) for x in range(QUAD)] for z in range(QUAD) for y in range(QUAD)]


def shift_fsdp(value, dy=0, dx=0):
    pairs = [
        (fsdp_index(z, y, x), fsdp_index(z, y + dy, x + dx))
        for z in range(QUAD)
        for y in range(QUAD)
        for x in range(QUAD)
    ]
    return lax.ppermute(value, "fsdp", pairs)


def shift_run(value, dz):
    pairs = [
        (z * 2 + core, ((z + dz) % QUAD) * 2 + core) for z in range(QUAD) for core in range(2)
    ]
    return lax.ppermute(value, "sp", pairs)


def other_core(value):
    return lax.ppermute(value, "sp", [(i, i ^ 1) for i in range(2 * QUAD)])


def exchange(value, axis, groups):
    return lax.all_to_all(value, axis, 0, 0, axis_index_groups=groups, tiled=True)


def gather(value, axis, groups):
    return exchange(jnp.broadcast_to(value[None], (QUAD,) + value.shape), axis, groups)


def prepare_kernel(
    step_ref,
    latents_ref,
    modulation_ref,
    base_qkv_ref,
    down_qkv_ref,
    up_qkv_ref,
    base_out_ref,
    down_out_ref,
    up_out_ref,
    slices_ref,
    merged_ref,
    by_x,
):
    for p in range(3):
        lowrank = jnp.dot(down_qkv_ref[p], up_qkv_ref[p], preferred_element_type=jnp.float32)
        merged_ref[p] = (base_qkv_ref[p].astype(jnp.float32) + lowrank).astype(jnp.bfloat16)
    lowrank = jnp.dot(up_out_ref[...], down_out_ref[...], preferred_element_type=jnp.float32)
    merged_ref[3] = (base_out_ref[...].astype(jnp.float32) + lowrank).astype(jnp.bfloat16)

    step = step_ref[0]
    shift = modulation_ref[0, pl.ds(step, 1), :]
    scale = modulation_ref[1, pl.ds(step, 1), :]
    latent = latents_ref[...].astype(jnp.float32)
    mean_square = jnp.mean(latent * latent, axis=-1, keepdims=True)
    normed = latent * lax.rsqrt(mean_square + EPSILON) * (1.0 + scale) + shift
    slab = normed.shape[1] // QUAD
    piece = slab // QUAD
    x_here = lax.axis_index("fsdp") % QUAD
    part = piece // QUAD
    for y in range(QUAD):
        for x in range(QUAD):
            starts = [z * slab + y * piece + x * part for z in range(QUAD)]
            by_x[x] = jnp.concatenate([normed[:, i : i + part] for i in starts], axis=1)
        turned = [by_x[lax.rem(x_here + k, QUAD)] for k in range(QUAD)]
        slices_ref[y] = jnp.concatenate(turned, axis=1).astype(jnp.bfloat16)


def attend_kernel(projected_ref, weights_ref, mine_ref, theirs_ref):
    projected = projected_ref[...]
    columns = projected.shape[1] // 3
    heads = []
    for h in range(columns // HEAD_DIM):
        queries, keys, values = (
            projected[:, p * columns + h * HEAD_DIM : p * columns + (h + 1) * HEAD_DIM]
            for p in range(3)
        )
        scores = lax.dot_general(
            queries, keys, (((1,), (1,)), ((), ())), preferred_element_type=jnp.float32
        ) * (1.0 / HEAD_DIM**0.5)
        weights = jnp.exp(scores - jnp.max(scores, axis=-1, keepdims=True))
        weights = weights / jnp.sum(weights, axis=-1, keepdims=True)
        heads.append(
            jnp.dot(
                weights.astype(jnp.bfloat16), values, preferred_element_type=jnp.float32
            ).astype(jnp.bfloat16)
        )
    attended = jnp.concatenate(heads, axis=1)
    half, slab = mine_ref.shape[0], weights_ref.shape[1]
    for k in range(QUAD):
        out = lax.dot_general(
            attended, weights_ref[k], (((1,), (1,)), ((), ())), preferred_element_type=jnp.float32
        ).astype(jnp.bfloat16)
        mine_ref[:, k * slab : (k + 1) * slab] = out[:half]
        theirs_ref[:, k * slab : (k + 1) * slab] = out[half:]


def finish_kernel(
    step_ref,
    own_ref,
    first_ref,
    second_ref,
    third_ref,
    latents_ref,
    noise_ref,
    modulation_ref,
    velocity_ref,
    next_ref,
):
    step = step_ref[0]
    block_out = own_ref[...].astype(jnp.float32)
    for ref in (first_ref, second_ref, third_ref):
        block_out = block_out + ref[...].astype(jnp.float32)
    piece = block_out.shape[1] // QUAD**3
    starts = [
        ((x * QUAD + y) * QUAD + z) * piece
        for z in range(QUAD)
        for y in range(QUAD)
        for x in range(QUAD)
    ]
    ordered = jnp.concatenate([block_out[:, i : i + piece] for i in starts], axis=1)
    gate = modulation_ref[2, pl.ds(step, 1), :]
    velocity = ((1.0 + gate) * ordered).astype(jnp.bfloat16)
    velocity_ref[...] = velocity
    position = jnp.full((1, 1), step, jnp.int32).astype(jnp.float32)
    step_size = plan_sigma(position + 1.0) - plan_sigma(position)
    next_ref[...] = (
        latents_ref[...].astype(jnp.float32)
        + step_size * velocity.astype(jnp.float32)
        + NOISE_LEVEL * jnp.sqrt(-step_size) * noise_ref[...].astype(jnp.float32)
    ).astype(jnp.bfloat16)


def hold_kernel(*refs):
    pass


def hold(values, earlier):
    held = pl.BlockSpec(memory_space=pl.ANY)
    return pl.pallas_call(
        hold_kernel,
        out_shape=[jax.ShapeDtypeStruct(x.shape, x.dtype) for x in values],
        in_specs=[held] * (len(values) + 1),
        out_specs=[held] * len(values),
        input_output_aliases={i: i for i in range(len(values))},
        cost_estimate=pl.CostEstimate(flops=4 * 10**9, bytes_accessed=0, transcendentals=0),
    )(*values, earlier)


def whole(shape):
    return pl.BlockSpec(shape, lambda i: (0,) * len(shape))


def call(kernel, out_shapes, *operands, scalars=0, mebibytes=20, scratch=()):
    smem = pl.BlockSpec(memory_space=pltpu.SMEM)
    return pl.pallas_call(
        kernel,
        grid=(1,),
        out_shape=out_shapes,
        in_specs=[smem] * scalars + [whole(x.shape) for x in operands[scalars:]],
        out_specs=jax.tree.map(lambda x: whole(x.shape), out_shapes),
        scratch_shapes=scratch,
        compiler_params=pltpu.CompilerParams(vmem_limit_bytes=mebibytes * 2**20),
    )(*operands)


def per_device(
    latents,
    step_noise,
    base_qkv,
    down_qkv,
    up_query_key_value,
    base_out,
    down_out,
    up_out,
    modulation,
    timestep,
):
    y = lax.axis_index("fsdp") // QUAD % QUAD
    rows, width = latents.shape[1:]
    part = base_qkv.shape[1]
    head_cols = base_qkv.shape[2]
    seq_len = rows * 2 * QUAD
    slab = width // QUAD

    slices, merged = call(
        prepare_kernel,
        (
            jax.ShapeDtypeStruct((QUAD, rows, slab), jnp.bfloat16),
            jax.ShapeDtypeStruct((4, part, head_cols), jnp.bfloat16),
        ),
        timestep,
        latents[0],
        modulation.transpose(1, 0, 2),
        base_qkv,
        down_qkv,
        up_query_key_value,
        base_out.T,
        down_out.T,
        up_out.T,
        scalars=1,
        mebibytes=60,
        scratch=[pltpu.VMEM((QUAD, rows, slab // QUAD), jnp.float32)],
    )

    mine = exchange(slices, "fsdp", Y_GROUPS)
    mine = jnp.concatenate([mine, mine], axis=0)
    mine = lax.rev(lax.dynamic_slice_in_dim(mine, y + 1, QUAD, 0), (0,))

    held = lax.all_gather(merged, "fsdp", axis_index_groups=Z_GROUPS, axis=0)

    moving = held[:, :3].transpose(0, 2, 1, 3).reshape(QUAD * part, 3 * head_cols)
    own_rows = held[:, 3].reshape(QUAD * part, head_cols)
    mine, moving = lax.optimization_barrier((mine, moving))
    blocks = [moving] + [shift_fsdp(moving, dx=-k) for k in range(1, QUAD)]

    run = jnp.stack([mine] + [shift_run(mine, k) for k in range(1, QUAD)], axis=1)

    out_rows = gather(own_rows, "fsdp", Y_GROUPS).reshape(slab, head_cols)
    copies = jnp.broadcast_to(out_rows[None], (QUAD, slab, head_cols))
    blocks = blocks[:1] + list(hold(blocks[1:], out_rows))
    out_rows = exchange(copies, "fsdp", X_GROUPS)
    weights = jnp.concatenate(blocks, axis=0)

    tokens = jnp.stack([run, other_core(run)], axis=1).reshape(QUAD * seq_len, slab)

    partial = jnp.dot(tokens, weights, preferred_element_type=jnp.float32).astype(jnp.bfloat16)
    partial = partial.reshape(QUAD, seq_len, 3 * head_cols)
    projected = partial[0].astype(jnp.float32)
    for k in (2, 1, 3):
        projected = projected + shift_fsdp(partial[k], dy=-k).astype(jnp.float32)
    projected = projected.astype(jnp.bfloat16)

    half = seq_len // 2
    ours, theirs = call(
        attend_kernel,
        (jax.ShapeDtypeStruct((half, width), jnp.bfloat16),) * 2,
        projected,
        out_rows,
    )
    pair = ours.astype(jnp.float32) + other_core(theirs).astype(jnp.float32)
    pair = pair.astype(jnp.bfloat16).reshape(QUAD, rows, width)
    returned = [pair[0]] + [shift_run(pair[k], -k) for k in (2, 1, 3)]
    velocity, next_rows = call(
        finish_kernel,
        (jax.ShapeDtypeStruct((rows, width), jnp.bfloat16),) * 2,
        timestep,
        *returned,
        latents[0],
        step_noise[0],
        modulation.transpose(1, 0, 2),
        scalars=1,
        mebibytes=20,
    )
    return (velocity[None], next_rows[None])


def solution(mesh):
    in_specs = (
        P("fsdp", "sp", None),
        P("fsdp", "sp", None),
        P(None, "fsdp", "sp"),
        P(None, "fsdp", None),
        P(None, None, "sp"),
        P("sp", "fsdp"),
        P("sp", None),
        P(None, "fsdp"),
        P(),
        P("fsdp"),
    )
    out_specs = (P("fsdp", "sp", None), P("fsdp", "sp", None))
    return jax.shard_map(
        per_device, mesh=mesh, in_specs=in_specs, out_specs=out_specs, check_vma=False
    )
```
